128 devices in a mesh: row: 16 (over x, z_lo, core), col: 8 (over y, z_hi).
Axes of the slice: x: 4, y: 4, z: 4 (z_hi: 2, z_lo: 2; z = z_hi * 2 + z_lo), core: 2. Of those that a mesh axis runs over, the one named last changes fastest.
Arguments:
- query_first: bfloat16 [3072, 8192], P('row', 'col'), may hold values from -180 to 180
- query_second: bfloat16 [3072, 8192], P('row', 'col'), may hold values from -180 to 180
- shared_key_states: bfloat16 [3072, 512], P('col', 'row'), may hold values from -7 to 7
- shared_value_states: bfloat16 [3072, 512], P('col', 'row'), may hold values from -6 to 6
- upstream_first: bfloat16 [3072, 8192], P('row', 'col'), may hold values from -6 to 6
- upstream_second: bfloat16 [3072, 8192], P('row', 'col'), may hold values from -6 to 6
- output_first: bfloat16 [3072, 8192], P('row', 'col'), may hold values from -6 to 6
- output_second: bfloat16 [3072, 8192], P('row', 'col'), may hold values from -6 to 6
- block_order: int32 [48], replicated, may hold values from 0 to 47, each once
Outputs:
- gradient_first: bfloat16 [3072, 8192], P('row', 'col')
- gradient_second: bfloat16 [3072, 8192], P('row', 'col')
- shared_key_gradient: bfloat16 [3072, 512], P('col', 'row')
- shared_value_gradient: bfloat16 [3072, 512], P('col', 'row')
The draws below stay inside these ranges and needn't reach their ends.
Inputs may be any that keep to these rules, and one draw needn't show every extreme that they name: A permutation of the 48 sequence blocks: storage block j holds the positions block_order[j] * 64 to block_order[j] * 64 + 63 in order.
All inputs are finite; a program needn't handle non-finite values.
Results may differ from the reference program's by a relative error of at most 0.0056.
Values may be sent and summed in bfloat16 or wider, within the bound.
No kernel may reach another device: no remote copies, remote signals or barrier semaphores. Data moves between devices by JAX's collectives and lax.ppermute only.
A program may use at most 192 MiB of HBM per device.

```python
import math
from functools import partial
import jax
import jax.numpy as jnp
from jax import lax

QUERY_HEADS = 64
SHARED_HEADS = 4
HEAD_SIZE = 128
BLK = 64
SEQUENCE_LENGTH = 3072
NBLK = 48


def shared_keys(key):
    return jnp.clip(jax.random.normal(key, (SEQUENCE_LENGTH, SHARED_HEADS * HEAD_SIZE), jnp.float32), -6.0, 6.0)


def drawn_queries(key):
    return jnp.clip(jax.random.normal(key, (SEQUENCE_LENGTH, QUERY_HEADS * HEAD_SIZE), jnp.float32), -6.0, 6.0)


def draw_query_first(key, part):
    key = jax.random.fold_in(key, 21)
    result = drawn_queries(key)
    return result.astype(jnp.bfloat16)


def draw_query_second(key, part):
    key = jax.random.fold_in(key, 33)
    result = drawn_queries(key)
    return result.astype(jnp.bfloat16)


def draw_shared_key_states(key, part):
    starting_offset = shared_keys(key)
    return starting_offset.astype(jnp.bfloat16)


def shard_levels(stream_key, dims, split, least, largest):
    factor_of, own = 1.0, jax.random.fold_in(stream_key, 6)
    for axis_at, blocks in split:
        heights = jnp.exp(jax.random.uniform(jax.random.fold_in(own, axis_at), (blocks,), jnp.float32, least / len(split), largest / len(split)))
        factor_of = factor_of * jnp.repeat(heights, dims[axis_at] // blocks).reshape([-1 if axis == axis_at else 1 for axis in range(len(dims))])
    return factor_of


def centred(stream_key, extent, deviation, reach, cuts=(), held_as=jnp.bfloat16):
    factor_of = shard_levels(stream_key, extent, cuts, -0.22, 0.18) if cuts else 1.0
    values = jax.random.normal(stream_key, extent, jnp.float32) * deviation * factor_of
    return jnp.minimum(jnp.maximum(values, -reach), reach).astype(held_as)


def setup_inputs(seed: int = 0) -> dict:
    keys = jax.random.split(jax.random.key(seed), 10)
    query_first = draw_query_first(jax.random.fold_in(keys[9], 71), 0)
    query_second = draw_query_second(jax.random.fold_in(keys[9], 71), 0)
    shared_key_states = draw_shared_key_states(jax.random.fold_in(keys[9], 71), 0)
    shared_value_states = centred(keys[3], (SEQUENCE_LENGTH, SHARED_HEADS * HEAD_SIZE), 1.0, 6.0, ((0, 8), (1, 16)))
    upstream_first = centred(keys[4], (SEQUENCE_LENGTH, QUERY_HEADS * HEAD_SIZE), 1.0, 6.0, ((0, 16), (1, 8)))
    upstream_second = centred(keys[5], (SEQUENCE_LENGTH, QUERY_HEADS * HEAD_SIZE), 1.0, 6.0, ((0, 16), (1, 8)))
    output_first = centred(keys[6], (SEQUENCE_LENGTH, QUERY_HEADS * HEAD_SIZE), 1.0, 6.0, ((0, 16), (1, 8)))
    output_second = centred(keys[7], (SEQUENCE_LENGTH, QUERY_HEADS * HEAD_SIZE), 1.0, 6.0, ((0, 16), (1, 8)))
    block_order = jax.random.permutation(keys[8], NBLK).astype(jnp.int32)
    return {"query_first": query_first, "query_second": query_second, "shared_key_states": shared_key_states, "shared_value_states": shared_value_states, "upstream_first": upstream_first, "upstream_second": upstream_second, "output_first": output_first, "output_second": output_second, "block_order": block_order}


def head_terms(inputs, allowed):
    query_head, upstream_head, output_head, key_head, value_head = inputs
    score_scale = 1.0 / math.sqrt(HEAD_SIZE)
    scores = jnp.dot(query_head, key_head.T, preferred_element_type=jnp.float32) * score_scale
    masked = jnp.where(allowed, scores, -jnp.inf)
    row_peak = lax.optimization_barrier(jnp.max(masked, axis=1, keepdims=True))
    row_total = lax.optimization_barrier(jnp.sum(jnp.exp(masked - row_peak), axis=1, keepdims=True))
    log_total = row_peak + jnp.log(row_total)
    weights = jnp.where(allowed, jnp.exp(scores - log_total), 0.0)
    slopes = jnp.dot(upstream_head, value_head.T, preferred_element_type=jnp.float32)
    row_delta = lax.optimization_barrier(jnp.sum(upstream_head.astype(jnp.float32) * output_head.astype(jnp.float32), axis=1, keepdims=True))
    dscore = (weights * (slopes - row_delta) * score_scale).astype(jnp.bfloat16)
    weights_low = weights.astype(jnp.bfloat16)
    query_grad = jnp.dot(dscore, key_head, preferred_element_type=jnp.float32)
    key_gradient_total = jnp.dot(dscore.T, query_head, preferred_element_type=jnp.float32)
    value_gradient_total = jnp.dot(weights_low.T, upstream_head, preferred_element_type=jnp.float32)
    return (query_grad, key_gradient_total, value_gradient_total)

def separate_heads(matrix, heads):
    return matrix.reshape(SEQUENCE_LENGTH, heads, HEAD_SIZE).transpose(1, 0, 2)

def layer_terms(queries, upstream, output, key_repeated, value_repeated, allowed):
    per_head_gradients = lax.map(partial(head_terms, allowed=allowed), (separate_heads(queries, QUERY_HEADS), separate_heads(upstream, QUERY_HEADS), separate_heads(output, QUERY_HEADS), key_repeated, value_repeated))
    query_grad = per_head_gradients[0].transpose(1, 0, 2).reshape(SEQUENCE_LENGTH, QUERY_HEADS * HEAD_SIZE)
    key_gradient_total = per_head_gradients[1].reshape(SHARED_HEADS, QUERY_HEADS // SHARED_HEADS, SEQUENCE_LENGTH, HEAD_SIZE).sum(axis=1)
    value_gradient_total = per_head_gradients[2].reshape(SHARED_HEADS, QUERY_HEADS // SHARED_HEADS, SEQUENCE_LENGTH, HEAD_SIZE).sum(axis=1)
    return (query_grad, key_gradient_total, value_gradient_total)

def reference(query_first, query_second, shared_key_states, shared_value_states, upstream_first, upstream_second, output_first, output_second, block_order):
    offsets = jnp.arange(BLK, dtype=jnp.int32)
    positions = (block_order[:, None] * BLK + offsets[None, :]).reshape(-1).astype(jnp.int32)
    allowed = positions[:, None] >= positions[None, :]
    key_repeated = jnp.repeat(separate_heads(shared_key_states, SHARED_HEADS), QUERY_HEADS // SHARED_HEADS, axis=0)
    value_repeated = jnp.repeat(separate_heads(shared_value_states, SHARED_HEADS), QUERY_HEADS // SHARED_HEADS, axis=0)
    grad_one, key_gradient_first, value_gradient_first = layer_terms(query_first, upstream_first, output_first, key_repeated, value_repeated, allowed)
    grad_two, key_gradient_second, value_gradient_second = layer_terms(query_second, upstream_second, output_second, key_repeated, value_repeated, allowed)
    shared_key_gradient = (key_gradient_first + key_gradient_second).transpose(1, 0, 2).reshape(SEQUENCE_LENGTH, SHARED_HEADS * HEAD_SIZE).astype(jnp.bfloat16)
    shared_value_gradient = (value_gradient_first + value_gradient_second).transpose(1, 0, 2).reshape(SEQUENCE_LENGTH, SHARED_HEADS * HEAD_SIZE).astype(jnp.bfloat16)
    return (grad_one.astype(jnp.bfloat16), grad_two.astype(jnp.bfloat16), shared_key_gradient, shared_value_gradient)
```

```python
import math

import jax
import jax.numpy as jnp
from jax import lax
from jax.experimental import pallas as pl
from jax.experimental.pallas import tpu as pltpu
from jax.sharding import Mesh
from jax.sharding import PartitionSpec as P

HEAD = 128
BLK = 64
CHUNK = 256
LADDER = (8, 4, 2, 1)
SCALE = 1.0 / math.sqrt(HEAD)
SCALE_LOG2 = SCALE * math.log2(math.e)
NEG = -1e30
SAFE = 2.0**60
F32 = jnp.float32
BF16 = jnp.bfloat16
AXES = ("x", "zl", "core", "y", "zh")


def nt(a, b):
    return lax.dot_general(a, b, (((1,), (1,)), ((), ())), preferred_element_type=F32)


def nn(a, b):
    return jnp.dot(a, b, preferred_element_type=F32)


def fold_rows(value, combine):
    return combine(value.reshape(value.shape[0] // 8, 8, value.shape[1]), axis=0)


def stacked(value):
    heads = value.shape[1] // HEAD
    return jnp.concatenate([value[:, h * HEAD : (h + 1) * HEAD] for h in range(heads)], axis=0)


def attention_kernel(order_ref, place_ref, *refs):
    piece_refs, own_refs, other_ref, refs = refs[:8], refs[8:14], refs[14], refs[15:]
    dq_own_ref, dq_other_ref, keep_ref, give_ref = refs[:4]
    wide_ref, k_ref, kt_ref, v_ref, s_ref, dk_ref, dv_ref, dqt_ref = refs[4:12]
    qs_ref, us_ref, peak_ref, total_ref, pieces_ref, rows_ref, sems = refs[12:]
    step = pl.program_id(0)
    steps = pl.num_programs(0)
    keys = k_ref.shape[0]
    blocks = keys // BLK
    lanes = s_ref.shape[1]
    core, x, z = [place_ref[i] for i in range(3)]

    def tile(start, t):
        return pl.ds(pl.multiple_of(start * t, t), t)

    def piece_copy(i):
        return pltpu.make_async_copy(piece_refs[i], pieces_ref.at[i], sems.at[i])

    def own_copy(i, layer=0):
        return pltpu.make_async_copy(own_refs[2 * i + layer], rows_ref.at[i], sems.at[8 + i])

    def other_copy():
        return pltpu.make_async_copy(other_ref, rows_ref.at[pl.ds(3, 3)], sems.at[11])

    @pl.when(step == 0)
    def _():
        for i in range(8):
            piece_copy(i).start()
        for layer in range(2):

            @pl.when(core == layer)
            def _(layer=layer):
                for i in range(3):
                    own_copy(i, layer).start()

        other_copy().start()
        for i in range(8):
            piece_copy(i).wait()
        for which in range(2):
            for side in range(2):
                core_at = core if side == 0 else 1 - core
                for dz in range(4):
                    z_at = (z + 4 - dz) % 4
                    sub = (z_at % 2) * 2 + core_at
                    for dx in range(4):
                        col = ((x + 4 - dx) % 4) * 2 + z_at // 2
                        wide_ref[tile(sub, 32), tile(col, 384)] = pieces_ref[
                            side * 4 + dz, dx, which
                        ].astype(F32)
            for t in range(keys // 128):
                part = wide_ref[:, t * 128 : (t + 1) * 128].T.astype(BF16)
                for half in range(2):
                    rows = part[half * BLK : half * BLK + BLK]
                    if which == 0:
                        k_ref[tile(order_ref[2 * t + half], BLK), :] = rows
                    else:
                        v_ref[tile(order_ref[2 * t + half], BLK), :HEAD] = rows
        for t in range(keys // 128):
            kt_ref[:, t * 128 : (t + 1) * 128] = (
                k_ref[t * 128 : (t + 1) * 128, :].astype(F32).T.astype(BF16)
            )
        lane = lax.broadcasted_iota(jnp.int32, (keys, HEAD), 1)
        v_ref[:, HEAD:] = jnp.where(lane < 3, -1.0, 0.0).astype(BF16)
        dk_ref[...] = jnp.zeros_like(dk_ref)
        dv_ref[...] = jnp.zeros_like(dv_ref)

    side = step // (steps // 2)

    @pl.when(step == 0)
    def _():
        for i in range(3):
            own_copy(i).wait()

    @pl.when(step == steps // 2)
    def _():
        other_copy().wait()

    block = tile(step % (steps // 2), BLK)
    query, upstream, output = [stacked(rows_ref[side * 3 + j, block, :]) for j in range(3)]
    delta = jnp.sum(upstream.astype(F32) * output.astype(F32), axis=1, keepdims=True)
    high = delta.astype(BF16).astype(F32)
    rest = delta - high
    middle = rest.astype(BF16).astype(F32)
    lane = lax.broadcasted_iota(jnp.int32, query.shape, 1)
    tail = jnp.where(
        lane == 0, high, jnp.where(lane == 1, middle, jnp.where(lane == 2, rest - middle, 0.0))
    )
    qs_ref[...] = query
    us_ref[:, :HEAD] = upstream
    us_ref[:, HEAD:] = tail.astype(BF16)

    row = (x * 2 + z % 2) * 2 + jnp.where(side == 0, core, 1 - core)
    own = order_ref[row * (steps // 2) + step % (steps // 2)]
    last = own // (CHUNK // BLK)

    def rows(base, size):
        return pl.ds(pl.multiple_of(base * CHUNK, CHUNK), size * CHUNK)

    def ladder(count, body):
        done = 0
        for size in LADDER:
            laps = (count - done) // size
            lax.fori_loop(
                0, laps, lambda j, c, done=done, size=size: (body(done + j * size, size), c)[1], 0
            )
            done = done + laps * size

    def edge():
        key_at = last * CHUNK + lax.broadcasted_iota(jnp.int32, (CHUNK, lanes), 0)
        query_at = own * BLK + lax.broadcasted_iota(jnp.int32, (CHUNK, lanes), 1) % BLK
        return jnp.where(query_at >= key_at, nt(k_ref[rows(last, 1), :], qs_ref[...]), NEG)

    def expo(scores, where):
        part = jnp.exp2((scores - peak_ref[...]) * SCALE_LOG2)
        s_ref[where, :] = part
        total_ref[...] += fold_rows(part, jnp.sum)

    def column_max(scores):
        return jnp.max(fold_rows(scores, jnp.max), axis=0, keepdims=True)

    def forward(scores):
        total_ref[...] = jnp.zeros_like(total_ref)
        expo(scores, rows(last, 1))
        ladder(
            last,
            lambda base, size: expo(nt(k_ref[rows(base, size), :], qs_ref[...]), rows(base, size)),
        )

    scores = edge()
    peak_ref[...] = column_max(scores)
    forward(scores)

    @pl.when(jnp.logical_not(jnp.max(total_ref[...]) < SAFE))
    def _():
        def widen(j, carry):
            scores = nt(k_ref[rows(j, 1), :], qs_ref[...])
            peak_ref[...] = jnp.maximum(peak_ref[...], column_max(scores))
            return carry

        lax.fori_loop(0, last, widen, 0)
        forward(edge())

    inverse = 1.0 / jnp.sum(total_ref[...], axis=0, keepdims=True)
    dqt_ref[...] = jnp.zeros_like(dqt_ref)

    def grads(base, size):
        at = rows(base, size)
        probs = s_ref[at, :] * inverse
        dscore = (probs * nt(v_ref[at, :], us_ref[...])).astype(BF16)
        dv_ref[at, :] += nn(probs.astype(BF16), us_ref[:, :HEAD])
        dk_ref[at, :] += nn(dscore, qs_ref[...])
        dqt_ref[...] += nn(kt_ref[:, at], dscore)

    ladder(last + 1, grads)

    dq = (dqt_ref[...] * SCALE).T.astype(BF16)
    for i, ref in enumerate((dq_own_ref, dq_other_ref)):

        @pl.when(side == i)
        def _(ref=ref):
            for h in range(lanes // BLK):
                ref[:, h * HEAD : (h + 1) * HEAD] = dq[h * BLK : (h + 1) * BLK]

    @pl.when(step == steps - 1)
    def _():
        for which in range(2):
            source = dk_ref if which == 0 else dv_ref
            for t in range(keys // 128):
                part = jnp.concatenate(
                    [source[tile(order_ref[2 * t + half], BLK), :] for half in range(2)], axis=0
                )
                if which == 0:
                    part = part * SCALE
                wide_ref[:, t * 128 : (t + 1) * 128] = part.T
            for b in range(4):
                for z_to in range(4):
                    slot = (b * 2 + z_to % 2) * 2 + z_to // 2
                    col = b * 2 + z_to // 2
                    for ref, core_to in ((keep_ref, core), (give_ref, 1 - core)):
                        sub = (z_to % 2) * 2 + core_to
                        ref[slot, which] = wide_ref[
                            tile(sub, 32), col * 384 : col * 384 + 384
                        ].astype(ref.dtype)


def attention(order, place, pieces, arrays):
    half = arrays[0].shape[0] // BLK
    heads = arrays[0].shape[1] // HEAD
    lanes = heads * BLK
    piece = pieces[0].shape
    keys = 8 * piece[-1]
    whole = lambda shape: pl.BlockSpec(shape, lambda i, *s: (0,) * len(shape))
    first = lambda i: jnp.minimum(i, half - 1)
    second = lambda i: jnp.maximum(i - half, 0)
    rows = (BLK, heads * HEAD)
    gradient = jax.ShapeDtypeStruct((half * BLK, heads * HEAD), BF16)
    parts = (16,) + piece[1:]
    return pl.pallas_call(
        attention_kernel,
        grid_spec=pltpu.PrefetchScalarGridSpec(
            num_scalar_prefetch=2,
            grid=(2 * half,),
            in_specs=[pl.BlockSpec(memory_space=pl.ANY)] * 15,
            out_specs=[
                pl.BlockSpec(rows, lambda i, *s: (first(i), 0)),
                pl.BlockSpec(rows, lambda i, *s: (second(i), 0)),
                whole(parts),
                whole(parts),
            ],
            scratch_shapes=[
                pltpu.VMEM((HEAD, keys), F32),
                pltpu.VMEM((keys, HEAD), BF16),
                pltpu.VMEM((HEAD, keys), BF16),
                pltpu.VMEM((keys, 2 * HEAD), BF16),
                pltpu.VMEM((keys, lanes), F32),
                pltpu.VMEM((keys, HEAD), F32),
                pltpu.VMEM((keys, HEAD), F32),
                pltpu.VMEM((HEAD, lanes), F32),
                pltpu.VMEM((lanes, HEAD), BF16),
                pltpu.VMEM((lanes, 2 * HEAD), BF16),
                pltpu.VMEM((1, lanes), F32),
                pltpu.VMEM((8, lanes), F32),
                pltpu.VMEM((8,) + piece, BF16),
                pltpu.VMEM((6,) + arrays[0].shape, BF16),
                pltpu.SemaphoreType.DMA((12,)),
            ],
        ),
        out_shape=[
            gradient,
            gradient,
            jax.ShapeDtypeStruct(parts, BF16),
            jax.ShapeDtypeStruct(parts, BF16),
        ],
        compiler_params=pltpu.CompilerParams(vmem_limit_bytes=56 * 1024 * 1024),
        name="attention",
    )(order, place, *pieces, *arrays)


def moved(value, target):
    def index(x, z, core, y):
        return (((x * 2 + z % 2) * 2 + core) * 4 + y) * 2 + z // 2

    pairs = [
        (index(x, z, core, y), index(*target(x, z, core, y)))
        for x in range(4)
        for z in range(4)
        for core in range(2)
        for y in range(4)
    ]
    return lax.ppermute(value, AXES, pairs)


def swap_cores(value):
    return lax.ppermute(value, "core", [(0, 1), (1, 0)])


def spread(piece):
    parts = jnp.stack(
        [moved(piece, lambda x, z, core, y, d=d: ((y + d) % 4, z, core, x)) for d in range(4)]
    )
    return [parts] + [
        moved(parts, lambda x, z, core, y, d=d: (x, (z + d) % 4, core, y)) for d in (1, 2, 3)
    ]


def reduce_pieces(keep, give):
    chip = (keep.astype(F32) + swap_cores(give).astype(F32)).astype(BF16)
    parts = lax.all_to_all(chip, ("x", "zl", "zh"), 0, 0)
    total = jnp.sum(parts.astype(F32), axis=0).astype(BF16)
    return moved(total, lambda x, z, core, y: (y, z, core, x))


def per_device(q1, q2, keys, values, u1, u2, o1, o2, block_order):
    x, core = lax.axis_index("x"), lax.axis_index("core")
    z = lax.axis_index("zh") * 2 + lax.axis_index("zl")
    place = jnp.stack([core, x, z]).astype(jnp.int32)
    own = (q1, q2, u1, u2, o1, o2)
    other = swap_cores(jnp.where(core == 0, jnp.stack(own[1::2]), jnp.stack(own[::2])))
    pieces = spread(jnp.stack([keys.T, values.T]))
    pieces = pieces + [swap_cores(piece) for piece in pieces]
    dq_own, dq_other, keep, give = attention(block_order, place, pieces, (*own, other))
    dq_back = swap_cores(dq_other)
    sums = reduce_pieces(keep, give)
    dq1 = jnp.where(core == 0, dq_own, dq_back)
    dq2 = jnp.where(core == 0, dq_back, dq_own)
    return dq1, dq2, sums[0].T, sums[1].T


def solution(mesh):
    split = Mesh(mesh.devices.reshape(4, 2, 2, 4, 2), AXES)
    row, col = ("x", "zl", "core"), ("y", "zh")
    wide, narrow = P(row, col), P(col, row)
    return jax.shard_map(
        per_device,
        mesh=split,
        in_specs=(wide, wide, narrow, narrow, wide, wide, wide, wide, P()),
        out_specs=(wide, wide, narrow, narrow),
        check_vma=False,
    )
```

```python
import math

import jax
import jax.numpy as jnp
from jax import lax
from jax.experimental import pallas as pl
from jax.experimental.pallas import tpu as pltpu
from jax.sharding import Mesh
from jax.sharding import PartitionSpec as P

HEAD = 128
BLK = 64
CHUNK = 256
LADDER = (8, 4, 2, 1)
SCALE = 1.0 / math.sqrt(HEAD)
SCALE_LOG2 = SCALE * math.log2(math.e)
NEG = -1e30
SAFE = 2.0**60
F32 = jnp.float32
BF16 = jnp.bfloat16
AXES = ("x", "zl", "core", "y", "zh")


def nt(a, b):
    return lax.dot_general(a, b, (((1,), (1,)), ((), ())), preferred_element_type=F32)


def nn(a, b):
    return jnp.dot(a, b, preferred_element_type=F32)


def fold_rows(value, combine):
    return combine(value.reshape(value.shape[0] // 8, 8, value.shape[1]), axis=0)


def stacked(value):
    heads = value.shape[1] // HEAD
    return jnp.concatenate([value[:, h * HEAD : (h + 1) * HEAD] for h in range(heads)], axis=0)


def attention_kernel(order_ref, place_ref, *refs):
    piece_refs, own_refs, other_ref, refs = refs[:8], refs[8:14], refs[14], refs[15:]
    dq_own_ref, dq_other_ref, keep_ref, give_ref = refs[:4]
    wide_ref, k_ref, kt_ref, v_ref, s_ref, dk_ref, dv_ref, dqt_ref = refs[4:12]
    qs_ref, us_ref, peak_ref, total_ref, pieces_ref, rows_ref, sems = refs[12:]
    step = pl.program_id(0)
    steps = pl.num_programs(0)
    keys = k_ref.shape[0]
    blocks = keys // BLK
    lanes = s_ref.shape[1]
    core, x, z = [place_ref[i] for i in range(3)]

    def tile(start, t):
        return pl.ds(pl.multiple_of(start * t, t), t)

    def piece_copy(i):
        return pltpu.make_async_copy(piece_refs[i], pieces_ref.at[i], sems.at[i])

    def own_copy(i, layer=0):
        return pltpu.make_async_copy(own_refs[2 * i + layer], rows_ref.at[i], sems.at[8 + i])

    def other_copy():
        return pltpu.make_async_copy(other_ref, rows_ref.at[pl.ds(3, 3)], sems.at[11])

    @pl.when(step == 0)
    def _():
        for i in range(8):
            piece_copy(i).start()
        for layer in range(2):

            @pl.when(core == layer)
            def _(layer=layer):
                for i in range(3):
                    own_copy(i, layer).start()

        for i in range(8):
            piece_copy(i).wait()
        other_copy().start()
        for which in range(2):
            for side in range(2):
                core_at = core if side == 0 else 1 - core
                for dz in range(4):
                    z_at = (z + 4 - dz) % 4
                    sub = (z_at % 2) * 2 + core_at
                    for dx in range(4):
                        col = ((x + 4 - dx) % 4) * 2 + z_at // 2
                        wide_ref[tile(sub, 32), tile(col, 384)] = pieces_ref[
                            side * 4 + dz, dx, which
                        ].astype(F32)
            for t in range(keys // 128):
                part = wide_ref[:, t * 128 : (t + 1) * 128].T.astype(BF16)
                for half in range(2):
                    rows = part[half * BLK : half * BLK + BLK]
                    if which == 0:
                        k_ref[tile(order_ref[2 * t + half], BLK), :] = rows
                    else:
                        v_ref[tile(order_ref[2 * t + half], BLK), :HEAD] = rows
        for t in range(keys // 128):
            kt_ref[:, t * 128 : (t + 1) * 128] = (
                k_ref[t * 128 : (t + 1) * 128, :].astype(F32).T.astype(BF16)
            )
        lane = lax.broadcasted_iota(jnp.int32, (keys, HEAD), 1)
        v_ref[:, HEAD:] = jnp.where(lane < 3, -1.0, 0.0).astype(BF16)
        dk_ref[...] = jnp.zeros_like(dk_ref)
        dv_ref[...] = jnp.zeros_like(dv_ref)

    side = step // (steps // 2)

    @pl.when(step == 0)
    def _():
        for i in range(3):
            own_copy(i).wait()

    @pl.when(step == steps // 2)
    def _():
        other_copy().wait()

    block = tile(step % (steps // 2), BLK)
    query, upstream, output = [stacked(rows_ref[side * 3 + j, block, :]) for j in range(3)]
    delta = jnp.sum(upstream.astype(F32) * output.astype(F32), axis=1, keepdims=True)
    high = delta.astype(BF16).astype(F32)
    rest = delta - high
    middle = rest.astype(BF16).astype(F32)
    lane = lax.broadcasted_iota(jnp.int32, query.shape, 1)
    tail = jnp.where(
        lane == 0, high, jnp.where(lane == 1, middle, jnp.where(lane == 2, rest - middle, 0.0))
    )
    qs_ref[...] = query
    us_ref[:, :HEAD] = upstream
    us_ref[:, HEAD:] = tail.astype(BF16)

    row = (x * 2 + z % 2) * 2 + jnp.where(side == 0, core, 1 - core)
    own = order_ref[row * (steps // 2) + step % (steps // 2)]
    last = own // (CHUNK // BLK)

    def rows(base, size):
        return pl.ds(pl.multiple_of(base * CHUNK, CHUNK), size * CHUNK)

    def ladder(count, body):
        done = 0
        for size in LADDER:
            laps = (count - done) // size
            lax.fori_loop(
                0, laps, lambda j, c, done=done, size=size: (body(done + j * size, size), c)[1], 0
            )
            done = done + laps * size

    def edge():
        key_at = last * CHUNK + lax.broadcasted_iota(jnp.int32, (CHUNK, lanes), 0)
        query_at = own * BLK + lax.broadcasted_iota(jnp.int32, (CHUNK, lanes), 1) % BLK
        return jnp.where(query_at >= key_at, nt(k_ref[rows(last, 1), :], qs_ref[...]), NEG)

    def expo(scores, where):
        part = jnp.exp2((scores - peak_ref[...]) * SCALE_LOG2)
        s_ref[where, :] = part
        total_ref[...] += fold_rows(part, jnp.sum)

    def column_max(scores):
        return jnp.max(fold_rows(scores, jnp.max), axis=0, keepdims=True)

    def forward(scores):
        total_ref[...] = jnp.zeros_like(total_ref)
        expo(scores, rows(last, 1))
        ladder(
            last,
            lambda base, size: expo(nt(k_ref[rows(base, size), :], qs_ref[...]), rows(base, size)),
        )

    scores = edge()
    peak_ref[...] = column_max(scores)
    forward(scores)

    @pl.when(jnp.logical_not(jnp.max(total_ref[...]) < SAFE))
    def _():
        def widen(j, carry):
            scores = nt(k_ref[rows(j, 1), :], qs_ref[...])
            peak_ref[...] = jnp.maximum(peak_ref[...], column_max(scores))
            return carry

        lax.fori_loop(0, last, widen, 0)
        forward(edge())

    inverse = 1.0 / jnp.sum(total_ref[...], axis=0, keepdims=True)
    dqt_ref[...] = jnp.zeros_like(dqt_ref)

    def grads(base, size):
        at = rows(base, size)
        probs = s_ref[at, :] * inverse
        dscore = (probs * nt(v_ref[at, :], us_ref[...])).astype(BF16)
        dv_ref[at, :] += nn(probs.astype(BF16), us_ref[:, :HEAD])
        dk_ref[at, :] += nn(dscore, qs_ref[...])
        dqt_ref[...] += nn(kt_ref[:, at], dscore)

    ladder(last + 1, grads)

    dq = (dqt_ref[...] * SCALE).T.astype(BF16)
    for i, ref in enumerate((dq_own_ref, dq_other_ref)):

        @pl.when(side == i)
        def _(ref=ref):
            for h in range(lanes // BLK):
                ref[:, h * HEAD : (h + 1) * HEAD] = dq[h * BLK : (h + 1) * BLK]

    @pl.when(step == steps - 1)
    def _():
        for which in range(2):
            source = dk_ref if which == 0 else dv_ref
            for t in range(keys // 128):
                part = jnp.concatenate(
                    [source[tile(order_ref[2 * t + half], BLK), :] for half in range(2)], axis=0
                )
                if which == 0:
                    part = part * SCALE
                wide_ref[:, t * 128 : (t + 1) * 128] = part.T
            for b in range(4):
                for z_to in range(4):
                    slot = (b * 2 + z_to % 2) * 2 + z_to // 2
                    col = b * 2 + z_to // 2
                    for ref, core_to in ((keep_ref, core), (give_ref, 1 - core)):
                        sub = (z_to % 2) * 2 + core_to
                        ref[slot, which] = wide_ref[
                            tile(sub, 32), col * 384 : col * 384 + 384
                        ].astype(ref.dtype)


def attention(order, place, pieces, arrays):
    half = arrays[0].shape[0] // BLK
    heads = arrays[0].shape[1] // HEAD
    lanes = heads * BLK
    piece = pieces[0].shape
    keys = 8 * piece[-1]
    first = lambda i: jnp.minimum(i, half - 1)
    second = lambda i: jnp.maximum(i - half, 0)
    rows = (BLK, heads * HEAD)
    gradient = jax.ShapeDtypeStruct((half * BLK, heads * HEAD), BF16)
    parts = (16,) + piece[1:]
    return pl.pallas_call(
        attention_kernel,
        grid_spec=pltpu.PrefetchScalarGridSpec(
            num_scalar_prefetch=2,
            grid=(2 * half,),
            in_specs=[pl.BlockSpec(memory_space=pl.ANY)] * 15,
            out_specs=[
                pl.BlockSpec(rows, lambda i, *s: (first(i), 0)),
                pl.BlockSpec(rows, lambda i, *s: (second(i), 0)),
                pl.BlockSpec(memory_space=pltpu.VMEM),
                pl.BlockSpec(memory_space=pltpu.VMEM),
            ],
            scratch_shapes=[
                pltpu.VMEM((HEAD, keys), F32),
                pltpu.VMEM((keys, HEAD), BF16),
                pltpu.VMEM((HEAD, keys), BF16),
                pltpu.VMEM((keys, 2 * HEAD), BF16),
                pltpu.VMEM((keys, lanes), F32),
                pltpu.VMEM((keys, HEAD), F32),
                pltpu.VMEM((keys, HEAD), F32),
                pltpu.VMEM((HEAD, lanes), F32),
                pltpu.VMEM((lanes, HEAD), BF16),
                pltpu.VMEM((lanes, 2 * HEAD), BF16),
                pltpu.VMEM((1, lanes), F32),
                pltpu.VMEM((8, lanes), F32),
                pltpu.VMEM((8,) + piece, BF16),
                pltpu.VMEM((6,) + arrays[0].shape, BF16),
                pltpu.SemaphoreType.DMA((12,)),
            ],
        ),
        out_shape=[
            gradient,
            gradient,
            pltpu.VMEM(parts, BF16),
            pltpu.VMEM(parts, BF16),
        ],
        compiler_params=pltpu.CompilerParams(vmem_limit_bytes=56 * 1024 * 1024),
        name="attention",
    )(order, place, *pieces, *arrays)


def moved(value, target):
    def index(x, z, core, y):
        return (((x * 2 + z % 2) * 2 + core) * 4 + y) * 2 + z // 2

    pairs = [
        (index(x, z, core, y), index(*target(x, z, core, y)))
        for x in range(4)
        for z in range(4)
        for core in range(2)
        for y in range(4)
    ]
    return lax.ppermute(value, AXES, pairs)


def swap_cores(value):
    return lax.ppermute(value, "core", [(0, 1), (1, 0)])


def spread(piece):
    parts = jnp.stack(
        [moved(piece, lambda x, z, core, y, d=d: ((y + d) % 4, z, core, x)) for d in range(4)]
    )
    return [parts] + [
        moved(parts, lambda x, z, core, y, d=d: (x, (z + d) % 4, core, y)) for d in (1, 2, 3)
    ]


def reduce_pieces(keep, give):
    chip = (keep.astype(F32) + swap_cores(give).astype(F32)).astype(BF16)
    parts = lax.all_to_all(chip, ("x", "zl", "zh"), 0, 0)
    total = jnp.sum(parts.astype(F32), axis=0).astype(BF16)
    return moved(total, lambda x, z, core, y: (y, z, core, x))


def per_device(q1, q2, keys, values, u1, u2, o1, o2, block_order):
    x, core = lax.axis_index("x"), lax.axis_index("core")
    z = lax.axis_index("zh") * 2 + lax.axis_index("zl")
    place = jnp.stack([core, x, z]).astype(jnp.int32)
    own = (q1, q2, u1, u2, o1, o2)
    other = swap_cores(jnp.where(core == 0, jnp.stack(own[1::2]), jnp.stack(own[::2])))
    pieces = spread(jnp.stack([keys.T, values.T]))
    pieces = pieces + [swap_cores(piece) for piece in pieces]
    dq_own, dq_other, keep, give = attention(block_order, place, pieces, (*own, other))
    dq_back = swap_cores(dq_other)
    sums = reduce_pieces(keep, give)
    dq1 = jnp.where(core == 0, dq_own, dq_back)
    dq2 = jnp.where(core == 0, dq_back, dq_own)
    return dq1, dq2, sums[0].T, sums[1].T


def solution(mesh):
    split = Mesh(mesh.devices.reshape(4, 2, 2, 4, 2), AXES)
    row, col = ("x", "zl", "core"), ("y", "zh")
    wide, narrow = P(row, col), P(col, row)
    return jax.shard_map(
        per_device,
        mesh=split,
        in_specs=(wide, wide, narrow, narrow, wide, wide, wide, wide, P()),
        out_specs=(wide, wide, narrow, narrow),
        check_vma=False,
    )
```

```python
import math

import jax
import jax.numpy as jnp
from jax import lax
from jax.experimental import pallas as pl
from jax.experimental.pallas import tpu as pltpu
from jax.sharding import Mesh
from jax.sharding import PartitionSpec as P

HEAD = 128
BLK = 64
CHUNK = 256
LADDER = (6, 4, 3, 2, 1)
SCALE = 1.0 / math.sqrt(HEAD)
SCALE_LOG2 = SCALE * math.log2(math.e)
NEG = -1e30
SAFE = 2.0**60
F32 = jnp.float32
BF16 = jnp.bfloat16
AXES = ("x", "zl", "core", "y", "zh")


def nt(a, b):
    return lax.dot_general(a, b, (((1,), (1,)), ((), ())), preferred_element_type=F32)


def nn(a, b):
    return jnp.dot(a, b, preferred_element_type=F32)


def fold_rows(value, combine):
    return combine(value.reshape(value.shape[0] // 8, 8, value.shape[1]), axis=0)


def stacked(value):
    heads = value.shape[1] // HEAD
    return jnp.concatenate([value[:, h * HEAD : (h + 1) * HEAD] for h in range(heads)], axis=0)


def attention_kernel(order_ref, place_ref, *refs):
    piece_refs, own_refs, other_ref, refs = refs[:8], refs[8:14], refs[14], refs[15:]
    dq_own_ref, dq_other_ref, keep_ref, give_ref = refs[:4]
    wide_ref, k_ref, kt_ref, v_ref, s_ref, dk_ref, dv_ref, dqt_ref = refs[4:12]
    qs_ref, us_ref, peak_ref, total_ref, pieces_ref, rows_ref, sems = refs[12:]
    step = pl.program_id(0)
    steps = pl.num_programs(0)
    keys = k_ref.shape[0]
    blocks = keys // BLK
    lanes = s_ref.shape[1]
    core, x, z = [place_ref[i] for i in range(3)]

    def tile(start, t):
        return pl.ds(pl.multiple_of(start * t, t), t)

    def piece_copy(i):
        return pltpu.make_async_copy(piece_refs[i], pieces_ref.at[i], sems.at[i])

    def own_copy(i, layer=0):
        return pltpu.make_async_copy(own_refs[2 * i + layer], rows_ref.at[i], sems.at[8 + i])

    def other_copy():
        return pltpu.make_async_copy(other_ref, rows_ref.at[pl.ds(3, 3)], sems.at[11])

    @pl.when(step == 0)
    def _():
        for i in range(8):
            piece_copy(i).start()
        for layer in range(2):

            @pl.when(core == layer)
            def _(layer=layer):
                for i in range(3):
                    own_copy(i, layer).start()

        for i in range(8):
            piece_copy(i).wait()
        other_copy().start()
        for which in range(2):
            for side in range(2):
                core_at = core if side == 0 else 1 - core
                for dz in range(4):
                    z_at = (z + 4 - dz) % 4
                    sub = (z_at % 2) * 2 + core_at
                    for dx in range(4):
                        col = ((x + 4 - dx) % 4) * 2 + z_at // 2
                        wide_ref[tile(sub, 32), tile(col, 384)] = pieces_ref[
                            side * 4 + dz, dx, which
                        ].astype(F32)
            for t in range(keys // 128):
                part = wide_ref[:, t * 128 : (t + 1) * 128].T.astype(BF16)
                for half in range(2):
                    rows = part[half * BLK : half * BLK + BLK]
                    if which == 0:
                        k_ref[tile(order_ref[2 * t + half], BLK), :] = rows
                    else:
                        v_ref[tile(order_ref[2 * t + half], BLK), :HEAD] = rows
        for t in range(keys // 128):
            kt_ref[:, t * 128 : (t + 1) * 128] = (
                k_ref[t * 128 : (t + 1) * 128, :].astype(F32).T.astype(BF16)
            )
        lane = lax.broadcasted_iota(jnp.int32, (keys, HEAD), 1)
        v_ref[:, HEAD:] = jnp.where(lane < 3, -1.0, 0.0).astype(BF16)
        dk_ref[...] = jnp.zeros_like(dk_ref)
        dv_ref[...] = jnp.zeros_like(dv_ref)

    side = step // (steps // 2)

    @pl.when(step == 0)
    def _():
        for i in range(3):
            own_copy(i).wait()

    @pl.when(step == steps // 2)
    def _():
        other_copy().wait()

    block = tile(step % (steps // 2), BLK)
    query, upstream, output = [stacked(rows_ref[side * 3 + j, block, :]) for j in range(3)]
    delta = jnp.sum(upstream.astype(F32) * output.astype(F32), axis=1, keepdims=True)
    high = delta.astype(BF16).astype(F32)
    rest = delta - high
    middle = rest.astype(BF16).astype(F32)
    lane = lax.broadcasted_iota(jnp.int32, query.shape, 1)
    tail = jnp.where(
        lane == 0, high, jnp.where(lane == 1, middle, jnp.where(lane == 2, rest - middle, 0.0))
    )
    qs_ref[...] = query
    us_ref[:, :HEAD] = upstream
    us_ref[:, HEAD:] = tail.astype(BF16)

    row = (x * 2 + z % 2) * 2 + jnp.where(side == 0, core, 1 - core)
    own = order_ref[row * (steps // 2) + step % (steps // 2)]
    last = own // (CHUNK // BLK)

    def rows(base, size):
        return pl.ds(pl.multiple_of(base * CHUNK, CHUNK), size * CHUNK)

    def ladder(count, body):
        done = 0
        for size in LADDER:
            laps = (count - done) // size
            lax.fori_loop(
                0, laps, lambda j, c, done=done, size=size: (body(done + j * size, size), c)[1], 0
            )
            done = done + laps * size

    def edge():
        key_at = last * CHUNK + lax.broadcasted_iota(jnp.int32, (CHUNK, lanes), 0)
        query_at = own * BLK + lax.broadcasted_iota(jnp.int32, (CHUNK, lanes), 1) % BLK
        return jnp.where(query_at >= key_at, nt(k_ref[rows(last, 1), :], qs_ref[...]), NEG)

    def expo(scores, where):
        part = jnp.exp2((scores - peak_ref[...]) * SCALE_LOG2)
        s_ref[where, :] = part
        total_ref[...] += fold_rows(part, jnp.sum)

    def column_max(scores):
        return jnp.max(fold_rows(scores, jnp.max), axis=0, keepdims=True)

    def forward(scores):
        total_ref[...] = jnp.zeros_like(total_ref)
        expo(scores, rows(last, 1))
        ladder(
            last,
            lambda base, size: expo(nt(k_ref[rows(base, size), :], qs_ref[...]), rows(base, size)),
        )

    scores = edge()
    peak_ref[...] = column_max(scores)
    forward(scores)

    @pl.when(jnp.logical_not(jnp.max(total_ref[...]) < SAFE))
    def _():
        def widen(j, carry):
            scores = nt(k_ref[rows(j, 1), :], qs_ref[...])
            peak_ref[...] = jnp.maximum(peak_ref[...], column_max(scores))
            return carry

        lax.fori_loop(0, last, widen, 0)
        forward(edge())

    inverse = 1.0 / jnp.sum(total_ref[...], axis=0, keepdims=True)
    dqt_ref[...] = jnp.zeros_like(dqt_ref)

    def grads(base, size):
        at = rows(base, size)
        probs = s_ref[at, :] * inverse
        dscore = (probs * nt(v_ref[at, :], us_ref[...])).astype(BF16)
        dv_ref[at, :] += nn(probs.astype(BF16), us_ref[:, :HEAD])
        dk_ref[at, :] += nn(dscore, qs_ref[...])
        dqt_ref[...] += nn(kt_ref[:, at], dscore)

    ladder(last + 1, grads)

    dq = (dqt_ref[...] * SCALE).T.astype(BF16)
    for i, ref in enumerate((dq_own_ref, dq_other_ref)):

        @pl.when(side == i)
        def _(ref=ref):
            for h in range(lanes // BLK):
                ref[:, h * HEAD : (h + 1) * HEAD] = dq[h * BLK : (h + 1) * BLK]

    @pl.when(step == steps - 1)
    def _():
        for which in range(2):
            source = dk_ref if which == 0 else dv_ref
            for t in range(keys // 128):
                part = jnp.concatenate(
                    [source[tile(order_ref[2 * t + half], BLK), :] for half in range(2)], axis=0
                )
                if which == 0:
                    part = part * SCALE
                wide_ref[:, t * 128 : (t + 1) * 128] = part.T
            for b in range(4):
                for z_to in range(4):
                    slot = (b * 2 + z_to % 2) * 2 + z_to // 2
                    col = b * 2 + z_to // 2
                    for ref, core_to in ((keep_ref, core), (give_ref, 1 - core)):
                        sub = (z_to % 2) * 2 + core_to
                        ref[slot, which] = wide_ref[
                            tile(sub, 32), col * 384 : col * 384 + 384
                        ].astype(ref.dtype)


def attention(order, place, pieces, arrays):
    half = arrays[0].shape[0] // BLK
    heads = arrays[0].shape[1] // HEAD
    lanes = heads * BLK
    piece = pieces[0].shape
    keys = 8 * piece[-1]
    first = lambda i: jnp.minimum(i, half - 1)
    second = lambda i: jnp.maximum(i - half, 0)
    rows = (BLK, heads * HEAD)
    gradient = jax.ShapeDtypeStruct((half * BLK, heads * HEAD), BF16)
    parts = (16,) + piece[1:]
    return pl.pallas_call(
        attention_kernel,
        grid_spec=pltpu.PrefetchScalarGridSpec(
            num_scalar_prefetch=2,
            grid=(2 * half,),
            in_specs=[pl.BlockSpec(memory_space=pl.ANY)] * 15,
            out_specs=[
                pl.BlockSpec(rows, lambda i, *s: (first(i), 0)),
                pl.BlockSpec(rows, lambda i, *s: (second(i), 0)),
                pl.BlockSpec(memory_space=pltpu.VMEM),
                pl.BlockSpec(memory_space=pltpu.VMEM),
            ],
            scratch_shapes=[
                pltpu.VMEM((HEAD, keys), F32),
                pltpu.VMEM((keys, HEAD), BF16),
                pltpu.VMEM((HEAD, keys), BF16),
                pltpu.VMEM((keys, 2 * HEAD), BF16),
                pltpu.VMEM((keys, lanes), F32),
                pltpu.VMEM((keys, HEAD), F32),
                pltpu.VMEM((keys, HEAD), F32),
                pltpu.VMEM((HEAD, lanes), F32),
                pltpu.VMEM((lanes, HEAD), BF16),
                pltpu.VMEM((lanes, 2 * HEAD), BF16),
                pltpu.VMEM((1, lanes), F32),
                pltpu.VMEM((8, lanes), F32),
                pltpu.VMEM((8,) + piece, BF16),
                pltpu.VMEM((6,) + arrays[0].shape, BF16),
                pltpu.SemaphoreType.DMA((12,)),
            ],
        ),
        out_shape=[
            gradient,
            gradient,
            pltpu.VMEM(parts, BF16),
            pltpu.VMEM(parts, BF16),
        ],
        compiler_params=pltpu.CompilerParams(vmem_limit_bytes=56 * 1024 * 1024),
        name="attention",
    )(order, place, *pieces, *arrays)


def moved(value, target):
    def index(x, z, core, y):
        return (((x * 2 + z % 2) * 2 + core) * 4 + y) * 2 + z // 2

    pairs = [
        (index(x, z, core, y), index(*target(x, z, core, y)))
        for x in range(4)
        for z in range(4)
        for core in range(2)
        for y in range(4)
    ]
    return lax.ppermute(value, AXES, pairs)


def swap_cores(value):
    return lax.ppermute(value, "core", [(0, 1), (1, 0)])


def spread(piece, other):
    parts = jnp.stack(
        [moved(piece, lambda x, z, core, y, d=d: ((y + d) % 4, z, core, x)) for d in range(4)]
    )
    parts, other = lax.optimization_barrier((parts, other))
    turns = [parts] + [
        moved(parts, lambda x, z, core, y, d=d: (x, (z + d) % 4, core, y)) for d in (1, 2, 3)
    ]
    return turns, other


def reduce_pieces(keep, give):
    z = lax.axis_index("zh") * 2 + lax.axis_index("zl")
    x = lax.axis_index("x")
    chip = keep.astype(F32) + swap_cores(give).astype(F32)
    chip = chip.reshape((4, 2, 2) + chip.shape[1:]).transpose(0, 2, 1, 3, 4, 5).reshape((4, 4) + chip.shape[1:])

    def take(value, k, axis):
        return lax.dynamic_index_in_dim(value, k % 4, axis, keepdims=False)

    low = chip.astype(BF16)
    total = take(low, z, 1).astype(F32)
    for d in (1, 2, 3):
        total = total + moved(take(low, z + d, 1), lambda x, z, core, y, d=d: (x, (z + d) % 4, core, y)).astype(F32)
    low = total.astype(BF16)
    return sum(
        moved(take(low, x + d, 0), lambda x, z, core, y, d=d: (y, z, core, (x + d) % 4)).astype(F32)
        for d in range(4)
    ).astype(BF16)


def per_device(q1, q2, keys, values, u1, u2, o1, o2, block_order):
    x, core = lax.axis_index("x"), lax.axis_index("core")
    z = lax.axis_index("zh") * 2 + lax.axis_index("zl")
    place = jnp.stack([core, x, z]).astype(jnp.int32)
    own = (q1, q2, u1, u2, o1, o2)
    other = swap_cores(jnp.where(core == 0, jnp.stack(own[1::2]), jnp.stack(own[::2])))
    pieces, other = spread(jnp.stack([keys.T, values.T]), other)
    pieces = pieces + [swap_cores(piece) for piece in pieces]
    dq_own, dq_other, keep, give = attention(block_order, place, pieces, (*own, other))
    dq_back = swap_cores(dq_other)
    sums = reduce_pieces(keep, give)
    dq1 = jnp.where(core == 0, dq_own, dq_back)
    dq2 = jnp.where(core == 0, dq_back, dq_own)
    return dq1, dq2, sums[0].T, sums[1].T


def solution(mesh):
    split = Mesh(mesh.devices.reshape(4, 2, 2, 4, 2), AXES)
    row, col = ("x", "zl", "core"), ("y", "zh")
    wide, narrow = P(row, col), P(col, row)
    return jax.shard_map(
        per_device,
        mesh=split,
        in_specs=(wide, wide, narrow, narrow, wide, wide, wide, wide, P()),
        out_specs=(wide, wide, narrow, narrow),
        check_vma=False,
    )
```
